512 devices in a mesh: seq: 32 (over x, y, core), mp: 16 (over z).
Axes of the slice: x: 4, y: 4, z: 16, core: 2. Of those that a mesh axis runs over, the one named last changes fastest.
Arguments:
- tokens: bfloat16 [4096, 4096], P('seq', 'mp'), may hold values from -10 to 10
- norm_gain: float32 [4096], replicated, may hold values from 0.1 to 1.9
- w_cand: bfloat16 [4096, 4096], P('seq', 'mp'), may hold values from -0.125 to 0.125
- w_gate: bfloat16 [4096, 4096], P('seq', 'mp'), may hold values from -0.046875 to 0.046875
- rec_gate: float32 [4096], P('mp'), may hold values from -0.75 to 0.75
- rec_cand: float32 [4096], P('mp'), may hold values from -0.6 to 0.6
- bias_gate: float32 [4096], P('mp')
- w_out: bfloat16 [4096, 4096], P('mp'), may hold values from -0.09375 to 0.09375
Outputs:
- output: bfloat16 [4096, 4096], P('seq', 'mp')
The draws below stay inside these ranges and needn't reach their ends.
All inputs are finite; a program needn't handle non-finite values.
Results may differ from the reference program's by a relative error of at most 0.0048.
Values may be sent and summed in bfloat16 or wider, within the bound.
No kernel may reach another device: no remote copies, remote signals or barrier semaphores. Data moves between devices by JAX's collectives and lax.ppermute only.
A program may use at most 64 MiB of HBM per device.

```python
import jax
import jax.numpy as jnp
from jax import lax

D = 4096
NEWTON = 3
LENGTH = 4096


def draw_bias_gate(key, part):
    first = jax.random.fold_in(key, 0)
    lowest = jnp.log(0.3 / LENGTH)
    highest = jnp.log(0.03)
    lograte = jax.random.uniform(first, (D,), jnp.float32, lowest, highest)
    rate = jnp.exp(lograte)
    return jnp.log((1.0 - rate) / rate)


def draw_tokens(key, part):
    first, second = jax.random.split(jax.random.fold_in(key, 71), 2)
    segment = (jnp.arange(LENGTH) * 8 // LENGTH).astype(jnp.int32)
    topics = 2.0 * jnp.clip(jax.random.normal(first, (8, D), jnp.float32), -2.5, 2.5)
    noise = jnp.clip(jax.random.normal(second, (LENGTH, D), jnp.float32), -3.0, 3.0)
    values = jnp.take(topics, segment, axis=0) + noise
    return jnp.clip(values, -10.0, 10.0).astype(jnp.bfloat16)


def levels(own_key, shape, cuts, low, largest):
    def one(position, blocks):
        draws = jax.random.uniform(jax.random.fold_in(jax.random.fold_in(own_key, 6), position), (blocks,), jnp.float32, low / len(cuts), largest / len(cuts))
        return jnp.repeat(jnp.exp(draws), shape[position] // blocks).reshape((-1,) + (1,) * (len(shape) - position - 1))

    loudness = one(*cuts[0])
    for cut in cuts[1:]:
        loudness = loudness * one(*cut)
    return loudness


def scatter_about(key, dims, deviation, limit, pieces=(), kind=jnp.bfloat16):
    values = jax.random.normal(key, dims, jnp.float32) * deviation
    if len(pieces) > 0:
        values = levels(key, dims, pieces, -0.22, 0.18) * values
    return jnp.clip(values, min=-limit, max=limit).astype(kind)


def setup_inputs(seed: int = 0) -> dict:
    streams_of = jax.random.split(jax.random.key(seed), 9)
    return {
        "tokens": draw_tokens(jax.random.fold_in(streams_of[8], 71), 0),
        "norm_gain": jnp.clip(1.0 + 0.18 * jax.random.normal(streams_of[1], (D,), jnp.float32), 0.1, 1.9),
        "w_cand": scatter_about(streams_of[2], (D, D), (D // 2) ** -0.5, 0.125, ((0, 32), (1, 16))),
        "w_gate": scatter_about(streams_of[3], (D, D), (4 * D) ** -0.5, 0.046875, ((0, 32), (1, 16))),
        "rec_gate": jnp.clip(jax.random.uniform(streams_of[4], (D,), jnp.float32, -0.75, 0.75) * levels(streams_of[4], (D,), ((0, 16),), -0.4, 0.0), -0.75, 0.75),
        "rec_cand": jnp.clip(jax.random.uniform(streams_of[5], (D,), jnp.float32, -0.6, 0.6) * levels(streams_of[5], (D,), ((0, 16),), -0.4, 0.0), -0.6, 0.6),
        "bias_gate": draw_bias_gate(jax.random.fold_in(streams_of[8], 71), 0),
        "w_out": scatter_about(streams_of[7], (D, D), D ** -0.5, 0.09375, ((0, 16),)),
    }


def compose(earlier, later):
    return (later[0] * earlier[0], later[0] * earlier[1] + later[1])

def cell(previous, cand_pre, gate_pre, rec_gate, rec_cand, bias_gate):
    gate = jax.nn.sigmoid(gate_pre + rec_gate * previous + bias_gate)
    cand = jnp.tanh(cand_pre + rec_cand * previous)
    value = gate * previous + (1.0 - gate) * cand
    slope = gate + gate * (1.0 - gate) * rec_gate * (previous - cand) + (1.0 - gate) * (1.0 - cand * cand) * rec_cand
    return (value, slope)

def reference(tokens, norm_gain, w_cand, w_gate, rec_gate, rec_cand, bias_gate, w_out):
    wide = tokens.astype(jnp.float32)
    factor = lax.rsqrt(lax.optimization_barrier(jnp.mean(wide * wide, axis=1, keepdims=True)) + 1e-05)
    normed = (wide * factor * norm_gain).astype(jnp.bfloat16)
    cand_pre = jnp.dot(normed, w_cand, preferred_element_type=jnp.float32)
    gate_pre = jnp.dot(normed, w_gate, preferred_element_type=jnp.float32)
    state = jnp.zeros(cand_pre.shape, jnp.float32)
    for newton_step in range(NEWTON):
        previous = jnp.concatenate([jnp.zeros((1, state.shape[1]), jnp.float32), state[:-1]], axis=0)
        value, slope = cell(previous, cand_pre, gate_pre, rec_gate, rec_cand, bias_gate)
        offset = value - slope * previous
        sweep = lax.associative_scan(compose, (slope, offset), axis=0)
        state = sweep[1]
    state_b = state.astype(jnp.bfloat16)
    return jnp.dot(state_b, w_out, preferred_element_type=jnp.float32).astype(jnp.bfloat16)
```

```python
import jax
import jax.numpy as jnp
from jax import lax
from jax.experimental import pallas as pl
from jax.experimental.pallas import tpu as pltpu
from jax.sharding import Mesh, PartitionSpec as P

NEWTON = 3
SEQ = ("x", "y", "c")
F32 = jnp.float32
BF16 = jnp.bfloat16
PARAMS = pltpu.CompilerParams(vmem_limit_bytes=48 * 1024 * 1024)


def project_kernel(lo_ref, hi_ref, gain_ref, w_ref, out_ref, factor_ref, acc_ref):
    step = pl.program_id(0)

    @pl.when(step == 0)
    def _():
        total = jnp.zeros((128, 256), F32)
        for ref in (lo_ref, hi_ref):
            for b in range(4):
                for a in range(2):
                    wide = ref[b, a].astype(F32)
                    total = total + wide * wide
        mean = jnp.sum(total, axis=1, keepdims=True) * (1.0 / 4096.0)
        factor_ref[...] = jnp.broadcast_to(lax.rsqrt(mean + 1e-05), (128, 256))

    def add(ref, a):
        factor = factor_ref[...]
        parts = []
        for b in range(4):
            wide = ref[b, a].astype(F32)
            gain = gain_ref[pl.ds(4 * step + b, 1), :]
            parts.append((wide * factor * gain).astype(BF16))
        normed = jnp.concatenate(parts, axis=1)
        return jnp.dot(normed, w_ref[...], preferred_element_type=F32)

    @pl.when(step == 0)
    def _():
        acc_ref[...] = add(lo_ref, 0)

    @pl.when(step == 1)
    def _():
        acc_ref[...] += add(lo_ref, 1)

    @pl.when(step == 2)
    def _():
        acc_ref[...] += add(hi_ref, 0)

    @pl.when(step == 3)
    def _():
        pre = (acc_ref[...] + add(hi_ref, 1)).T
        out_ref[:, 0:8, :] = pre[:256].reshape(32, 8, 128)
        out_ref[:, 8:16, :] = pre[256:].reshape(32, 8, 128)


def project(lo, hi, gain, weights):
    whole = pl.BlockSpec((4, 2, 128, 256), lambda i: (0, 0, 0, 0))
    return pl.pallas_call(
        project_kernel,
        grid=(4,),
        in_specs=[
            whole,
            whole,
            pl.BlockSpec((16, 256), lambda i: (0, 0)),
            pl.BlockSpec((1024, 512), lambda i: (i, 0)),
        ],
        out_specs=pl.BlockSpec((32, 16, 128), lambda i: (0, 0, 0)),
        out_shape=jax.ShapeDtypeStruct((32, 16, 128), F32),
        scratch_shapes=[pltpu.VMEM((128, 256), F32), pltpu.VMEM((128, 512), F32)],
        compiler_params=PARAMS,
        name="project",
    )(lo, hi, gain, weights)


def newton_kernel(pre_ref, par_ref, out_ref, cand_ref, gate_ref):
    rec_gate, rec_cand, bias = par_ref[0:1, :], par_ref[1:2, :], par_ref[2:3, :]
    for half in range(2):
        cand_ref[half] = pre_ref[16 * half : 16 * half + 16, 0:8, :].reshape(128, 128).T
        gate_ref[half] = pre_ref[16 * half : 16 * half + 16, 8:16, :].reshape(128, 128).T
    row = lax.broadcasted_iota(jnp.int32, (8, 256), 0)
    lane = lax.broadcasted_iota(jnp.int32, (8, 256), 1)

    def tokens_of(ref, r):
        picked = pl.ds(r, 8, stride=16)
        return jnp.concatenate([ref[0, picked, :], ref[1, picked, :]], axis=1)

    def shifted(a, b, by, axis):
        inside = (row if axis == 0 else lane) >= by
        return (
            jnp.where(inside, pltpu.roll(a, by, axis), 1.0),
            jnp.where(inside, pltpu.roll(b, by, axis), 0.0),
        )

    def entering(a, b):
        for by in (1, 2, 4):
            ea, eb = shifted(a, b, by, 0)
            a, b = a * ea, a * eb + b
        ta = jnp.broadcast_to(a[7:8, :], (8, 256))
        tb = jnp.broadcast_to(b[7:8, :], (8, 256))
        for by in (8, 16, 32, 64, 128):
            ea, eb = shifted(ta, tb, by, 1)
            ta, tb = ta * ea, ta * eb + tb
        carried = jnp.where(lane >= 8, pltpu.roll(tb, 8, 1), 0.0)
        ea, eb = shifted(a, b, 1, 0)
        return ea * carried + eb

    state = [jnp.zeros((8, 256), F32)] * 16
    carry = jnp.zeros((8, 256), F32)
    for _ in range(NEWTON):
        sweep = []
        for r in range(16):
            previous = carry if r == 0 else state[r - 1]
            cand_pre = tokens_of(cand_ref, r)
            gate_pre = tokens_of(gate_ref, r)
            gate = jax.nn.sigmoid(gate_pre + rec_gate * previous + bias)
            cand = jnp.tanh(cand_pre + rec_cand * previous)
            rest = 1.0 - gate
            value = gate * previous + rest * cand
            slope = (
                gate
                + gate * rest * rec_gate * (previous - cand)
                + rest * (1.0 - cand * cand) * rec_cand
            )
            offset = value - slope * previous
            if r > 0:
                slope, offset = slope * sweep[-1][0], slope * sweep[-1][1] + offset
            sweep.append((slope, offset))
        carry = entering(*sweep[-1])
        state = [a * carry + b for a, b in sweep]
    for r in range(16):
        for half in range(2):
            gate_ref[half, pl.ds(r, 8, stride=16), :] = state[r][:, 128 * half : 128 * half + 128]
    turned = jnp.concatenate([gate_ref[0].T, gate_ref[1].T], axis=0).reshape(32, 1, 8, 128)
    out_ref[...] = jnp.broadcast_to(turned, (32, 4, 8, 128)).reshape(1024, 128).astype(BF16)


def newton(pre, par):
    return pl.pallas_call(
        newton_kernel,
        out_shape=jax.ShapeDtypeStruct((1024, 128), BF16),
        scratch_shapes=[pltpu.VMEM((2, 128, 128), F32)] * 2,
        compiler_params=PARAMS,
        name="newton",
    )(pre, par)


def output_kernel(core_ref, state_ref, own_ref, peer_ref, out_ref, rows_ref):
    wide = state_ref[...].astype(F32).reshape(32, 4, 8, 128)
    mine = core_ref[0]
    for b in range(4):
        rows_ref[b] = wide[:, b].reshape(256, 128)
    own, peer = [], []
    for b in range(4):
        own.append(rows_ref[b, pl.ds(pl.multiple_of(mine * 128, 128), 128), :].T)
        peer.append(rows_ref[b, pl.ds(pl.multiple_of((1 - mine) * 128, 128), 128), :].T)
    left = jnp.concatenate(own + peer, axis=1).astype(BF16)
    for a in range(4):
        columns = pl.ds(256 * a, 256)
        right = jnp.concatenate(
            [own_ref[:, :, columns].reshape(512, 256), peer_ref[:, :, columns].reshape(512, 256)], axis=0
        )
        out_ref[a] = jnp.dot(left, right, preferred_element_type=F32).astype(BF16)


def output(core, state, own, peer):
    vmem = pl.BlockSpec(memory_space=pltpu.VMEM)
    return pl.pallas_call(
        output_kernel,
        in_specs=[pl.BlockSpec(memory_space=pltpu.SMEM), vmem, vmem, vmem],
        out_specs=vmem,
        out_shape=jax.ShapeDtypeStruct((4, 128, 256), BF16),
        scratch_shapes=[pltpu.VMEM((4, 256, 128), F32)],
        compiler_params=PARAMS,
        name="output",
    )(core, state, own, peer)


def per_device(tokens, norm_gain, w_cand, w_gate, rec_gate, rec_cand, bias_gate, w_out):
    core = lax.axis_index("c")
    mine = lax.axis_index(SEQ)
    weights = lax.all_gather(jnp.concatenate([w_cand, w_gate], axis=1), SEQ, axis=0, tiled=True)

    far = lax.all_gather(tokens, "za", axis=0)
    lo = lax.all_gather(far[:2], "zb", axis=0)
    hi = lax.all_gather(far[2:], "zb", axis=0)

    half = lax.dynamic_slice(w_out, (core * 128, 0), (128, 4096))
    half = half.reshape(128, 4, 4, 256).transpose(2, 0, 1, 3).reshape(4, 128, 1024)
    half, lo, hi = lax.optimization_barrier((half, lo, hi))
    own = lax.all_to_all(half, "zb", 0, 0, tiled=True)
    peer = lax.ppermute(own, "c", [(0, 1), (1, 0)])

    par = jnp.stack([rec_gate, rec_cand, bias_gate])
    par = jnp.tile(lax.dynamic_slice(par, (0, mine * 8), (3, 8)), (1, 32))

    pre = project(lo, hi, norm_gain.reshape(16, 256), weights)
    pre = lax.all_to_all(pre, SEQ, 0, 0, tiled=True)
    state = newton(pre, par)
    state = lax.all_to_all(state.reshape(128, 8, 128), SEQ + ("zb",), 0, 0, tiled=True)
    sums = output(core.reshape(1), state.reshape(1024, 128), own, peer)
    sums = lax.all_to_all(sums, "za", 0, 0, tiled=True)
    return jnp.sum(sums.astype(F32), axis=0).astype(BF16)


def solution(mesh):
    fine = Mesh(mesh.devices.reshape(4, 4, 2, 4, 4), ("x", "y", "c", "za", "zb"))
    z = ("za", "zb")
    placed = (P(SEQ, z), P(), P(SEQ, z), P(SEQ, z), P(z), P(z), P(z), P(z, None))
    return jax.shard_map(per_device, mesh=fine, in_specs=placed, out_specs=P(SEQ, z), check_vma=False)
```

```python
import jax
import jax.numpy as jnp
from jax import lax
from jax.experimental import pallas as pl
from jax.experimental.pallas import tpu as pltpu
from jax.sharding import Mesh, PartitionSpec as P

NEWTON = 3
SEQ = ("x", "y", "c")
F32 = jnp.float32
BF16 = jnp.bfloat16
PARAMS = pltpu.CompilerParams(vmem_limit_bytes=48 * 1024 * 1024)


SHIFTS = (0, 1, 3, 2)


def pick_kernel(place_ref, w_ref, own_ref, *outs):
    near, core = place_ref[0], place_ref[1]
    for a in range(4):
        columns = pl.ds(pl.multiple_of((4 * a + near) * 256, 256), 256)
        own_ref[a] = w_ref[:, columns]
    rows = pl.ds(pl.multiple_of(core * 128, 128), 128)
    for out_ref, shift in zip(outs, SHIFTS[1:]):
        for a in range(4):
            block = 4 * a + lax.rem(near + shift, 4)
            out_ref[a] = w_ref[rows, pl.ds(pl.multiple_of(block * 256, 256), 256)]


def pick(place, w_out):
    vmem = pl.BlockSpec(memory_space=pltpu.VMEM)
    shapes = [(4, 256, 256)] + [(4, 128, 256)] * 3
    return pl.pallas_call(
        pick_kernel,
        in_specs=[pl.BlockSpec(memory_space=pltpu.SMEM), vmem],
        out_specs=[vmem] * 4,
        out_shape=[jax.ShapeDtypeStruct(shape, BF16) for shape in shapes],
        compiler_params=PARAMS,
        name="pick",
    )(place, w_out)


def norm_kernel(place_ref, own_ref, up_ref, down_ref, two_ref, gain_ref, out_ref):
    refs = (own_ref, up_ref, down_ref, two_ref)
    total = jnp.zeros((128, 256), F32)
    for ref in refs:
        for a in range(4):
            wide = ref[a].astype(F32)
            total = total + wide * wide
    mean = jnp.sum(total, axis=1, keepdims=True) * (1.0 / 4096.0)
    factor = jnp.broadcast_to(lax.rsqrt(mean + 1e-05), (128, 256))
    for ref, shift in zip(refs, SHIFTS):
        near = lax.rem(place_ref[0] + 4 - shift, 4)
        for a in range(4):
            block = 4 * a + near
            gain = gain_ref[pl.ds(block, 1), :]
            out_ref[block] = (ref[a].astype(F32) * factor * gain).astype(BF16)


def norm(place, blocks, gain):
    vmem = pl.BlockSpec(memory_space=pltpu.VMEM)
    return pl.pallas_call(
        norm_kernel,
        in_specs=[pl.BlockSpec(memory_space=pltpu.SMEM)] + [vmem] * 5,
        out_specs=vmem,
        out_shape=jax.ShapeDtypeStruct((16, 128, 256), BF16),
        compiler_params=PARAMS,
        name="norm",
    )(place, *blocks, gain)


def project_kernel(normed_ref, w_ref, out_ref, acc_ref):
    step = pl.program_id(0)
    normed = jnp.concatenate([normed_ref[b] for b in range(4)], axis=1)
    part = jnp.dot(normed, w_ref[...], preferred_element_type=F32)

    @pl.when(step == 0)
    def _():
        acc_ref[...] = part

    @pl.when((step > 0) & (step < 3))
    def _():
        acc_ref[...] += part

    @pl.when(step == 3)
    def _():
        pre = (acc_ref[...] + part).T
        out_ref[:, 0:8, :] = pre[:256].reshape(32, 8, 128)
        out_ref[:, 8:16, :] = pre[256:].reshape(32, 8, 128)


def project(normed, weights):
    return pl.pallas_call(
        project_kernel,
        grid=(4,),
        in_specs=[
            pl.BlockSpec((4, 128, 256), lambda i: (i, 0, 0)),
            pl.BlockSpec((1024, 512), lambda i: (i, 0)),
        ],
        out_specs=pl.BlockSpec((32, 16, 128), lambda i: (0, 0, 0)),
        out_shape=jax.ShapeDtypeStruct((32, 16, 128), F32),
        scratch_shapes=[pltpu.VMEM((128, 512), F32)],
        compiler_params=PARAMS,
        name="project",
    )(normed, weights)


def newton_kernel(pre_ref, par_ref, out_ref, cand_ref, gate_ref):
    rec_gate, rec_cand, bias = par_ref[0:1, :], par_ref[1:2, :], par_ref[2:3, :]
    for half in range(2):
        cand_ref[half] = pre_ref[16 * half : 16 * half + 16, 0:8, :].reshape(128, 128).T
        gate_ref[half] = pre_ref[16 * half : 16 * half + 16, 8:16, :].reshape(128, 128).T
    row = lax.broadcasted_iota(jnp.int32, (8, 256), 0)
    lane = lax.broadcasted_iota(jnp.int32, (8, 256), 1)

    def tokens_of(ref, r):
        picked = pl.ds(r, 8, stride=16)
        return jnp.concatenate([ref[0, picked, :], ref[1, picked, :]], axis=1)

    def shifted(a, b, by, axis):
        inside = (row if axis == 0 else lane) >= by
        return (
            jnp.where(inside, pltpu.roll(a, by, axis), 1.0),
            jnp.where(inside, pltpu.roll(b, by, axis), 0.0),
        )

    def entering(a, b):
        for by in (1, 2, 4):
            ea, eb = shifted(a, b, by, 0)
            a, b = a * ea, a * eb + b
        ta = jnp.broadcast_to(a[7:8, :], (8, 256))
        tb = jnp.broadcast_to(b[7:8, :], (8, 256))
        for by in (8, 16, 32, 64, 128):
            ea, eb = shifted(ta, tb, by, 1)
            ta, tb = ta * ea, ta * eb + tb
        carried = jnp.where(lane >= 8, pltpu.roll(tb, 8, 1), 0.0)
        ea, eb = shifted(a, b, 1, 0)
        return ea * carried + eb

    state = [jnp.zeros((8, 256), F32)] * 16
    carry = jnp.zeros((8, 256), F32)
    for _ in range(NEWTON):
        sweep = []
        for r in range(16):
            previous = carry if r == 0 else state[r - 1]
            cand_pre = tokens_of(cand_ref, r)
            gate_pre = tokens_of(gate_ref, r)
            gate = jax.nn.sigmoid(gate_pre + rec_gate * previous + bias)
            cand = jnp.tanh(cand_pre + rec_cand * previous)
            rest = 1.0 - gate
            value = gate * previous + rest * cand
            slope = (
                gate
                + gate * rest * rec_gate * (previous - cand)
                + rest * (1.0 - cand * cand) * rec_cand
            )
            offset = value - slope * previous
            if r > 0:
                slope, offset = slope * sweep[-1][0], slope * sweep[-1][1] + offset
            sweep.append((slope, offset))
        carry = entering(*sweep[-1])
        state = [a * carry + b for a, b in sweep]
    for r in range(16):
        for half in range(2):
            gate_ref[half, pl.ds(r, 8, stride=16), :] = state[r][:, 128 * half : 128 * half + 128]
    turned = jnp.concatenate([gate_ref[0].T, gate_ref[1].T], axis=0).reshape(32, 1, 8, 128)
    out_ref[...] = jnp.broadcast_to(turned, (32, 4, 8, 128)).reshape(1024, 128).astype(BF16)


def newton(pre, par):
    return pl.pallas_call(
        newton_kernel,
        out_shape=jax.ShapeDtypeStruct((1024, 128), BF16),
        scratch_shapes=[pltpu.VMEM((2, 128, 128), F32)] * 2,
        compiler_params=PARAMS,
        name="newton",
    )(pre, par)


def output_kernel(place_ref, state_ref, own_ref, mine_ref, peer_ref, out_ref, kept_ref, rows_ref):
    near, core, far = place_ref[0], place_ref[1], place_ref[2]
    wide = state_ref[...].astype(F32).reshape(32, 4, 8, 128)
    for b in range(4):
        rows_ref[b] = wide[:, b].reshape(256, 128)
    left = [rows_ref[near].T]
    for half in (core, 1 - core):
        rows = pl.ds(pl.multiple_of(half * 128, 128), 128)
        left += [rows_ref[lax.rem(near + 4 - shift, 4), rows, :].T for shift in SHIFTS[1:]]
    left = jnp.concatenate(left, axis=1).astype(BF16)
    for a in range(4):
        right = [own_ref[a]] + [ref[d, a] for ref in (mine_ref, peer_ref) for d in range(3)]
        part = jnp.dot(left, jnp.concatenate(right, axis=0), preferred_element_type=F32)
        out_ref[a] = part.astype(BF16)

        @pl.when(far == a)
        def _():
            kept_ref[...] = part


def output(place, state, own, mine, peer):
    vmem = pl.BlockSpec(memory_space=pltpu.VMEM)
    return pl.pallas_call(
        output_kernel,
        in_specs=[pl.BlockSpec(memory_space=pltpu.SMEM)] + [vmem] * 4,
        out_specs=[vmem] * 2,
        out_shape=[
            jax.ShapeDtypeStruct((4, 128, 256), BF16),
            jax.ShapeDtypeStruct((128, 256), F32),
        ],
        scratch_shapes=[pltpu.VMEM((4, 256, 128), F32)],
        compiler_params=PARAMS,
        name="output",
    )(place, state, own, mine, peer)


def total_kernel(place_ref, kept_ref, sums_ref, out_ref):
    total = kept_ref[...]
    for a in range(4):
        total = total + jnp.where(place_ref[2] == a, 0.0, sums_ref[a].astype(F32))
    out_ref[...] = total.astype(BF16)


def total(place, kept, sums):
    vmem = pl.BlockSpec(memory_space=pltpu.VMEM)
    return pl.pallas_call(
        total_kernel,
        in_specs=[pl.BlockSpec(memory_space=pltpu.SMEM), vmem, vmem],
        out_specs=vmem,
        out_shape=jax.ShapeDtypeStruct((128, 256), BF16),
        compiler_params=PARAMS,
        name="total",
    )(place, kept, sums)


def moved(array, axes, size, shift):
    return lax.ppermute(array, axes, [(i, (i + shift) % size) for i in range(size)])


def per_device(tokens, norm_gain, w_cand, w_gate, rec_gate, rec_cand, bias_gate, w_out):
    place = jnp.stack([lax.axis_index(axis) for axis in ("zb", "c", "za")])
    mine = lax.axis_index(SEQ)
    weights = lax.all_gather(jnp.concatenate([w_cand, w_gate], axis=1), SEQ, axis=0, tiled=True)

    far = lax.all_gather(tokens, "za", axis=0)
    own, *parts = pick(place, w_out)
    *parts, far = lax.optimization_barrier((*parts, far))
    blocks = [far] + [moved(far, ("za", "zb"), 16, shift) for shift in (1, 15, 2)]
    parts = [moved(part, "zb", 4, shift) for part, shift in zip(parts, SHIFTS[1:])]
    normed = norm(place, blocks, norm_gain.reshape(16, 256))
    *parts, normed = lax.optimization_barrier((*parts, normed))
    half = jnp.stack(parts)
    peer = lax.ppermute(half, "c", [(0, 1), (1, 0)])

    par = jnp.stack([rec_gate, rec_cand, bias_gate])
    par = jnp.tile(lax.dynamic_slice(par, (0, mine * 8), (3, 8)), (1, 32))

    pre = project(normed, weights)
    pre = lax.all_to_all(pre, SEQ, 0, 0, tiled=True)
    state = newton(pre, par)
    state = lax.all_to_all(state.reshape(128, 8, 128), SEQ + ("zb",), 0, 0, tiled=True)
    sums, kept = output(place, state.reshape(1024, 128), own, half, peer)
    sums = lax.all_to_all(sums, "za", 0, 0, tiled=True)
    return total(place, kept, sums)


def solution(mesh):
    fine = Mesh(mesh.devices.reshape(4, 4, 2, 4, 4), ("x", "y", "c", "za", "zb"))
    z = ("za", "zb")
    placed = (P(SEQ, z), P(), P(SEQ, z), P(SEQ, z), P(z), P(z), P(z), P(z, None))
    return jax.shard_map(per_device, mesh=fine, in_specs=placed, out_specs=P(SEQ, z), check_vma=False)
```

```python
import jax
import jax.numpy as jnp
from jax import lax
from jax.experimental import pallas as pl
from jax.experimental.pallas import tpu as pltpu
from jax.sharding import Mesh, PartitionSpec as P

NEWTON = 3
SEQ = ("x", "y", "c")
F32 = jnp.float32
BF16 = jnp.bfloat16
PARAMS = pltpu.CompilerParams(vmem_limit_bytes=48 * 1024 * 1024)


SHIFTS = (0, 1, 3, 2)


def pick_kernel(place_ref, w_ref, own_ref, *outs):
    near, core = place_ref[0], place_ref[1]
    for a in range(4):
        columns = pl.ds(pl.multiple_of((4 * a + near) * 256, 256), 256)
        own_ref[a] = w_ref[:, columns]
    rows = pl.ds(pl.multiple_of(core * 128, 128), 128)
    for out_ref, shift in zip(outs, SHIFTS[1:]):
        for a in range(4):
            block = 4 * a + lax.rem(near + shift, 4)
            out_ref[a] = w_ref[rows, pl.ds(pl.multiple_of(block * 256, 256), 256)]


def pick(place, w_out):
    vmem = pl.BlockSpec(memory_space=pltpu.VMEM)
    shapes = [(4, 256, 256)] + [(4, 128, 256)] * 3
    return pl.pallas_call(
        pick_kernel,
        in_specs=[pl.BlockSpec(memory_space=pltpu.SMEM), vmem],
        out_specs=[vmem] * 4,
        out_shape=[jax.ShapeDtypeStruct(shape, BF16) for shape in shapes],
        compiler_params=PARAMS,
        name="pick",
    )(place, w_out)


def norm_kernel(place_ref, own_ref, up_ref, down_ref, two_ref, gain_ref, keep_ref, give_ref):
    refs = (own_ref, up_ref, down_ref, two_ref)
    first = place_ref[1] == 0
    total = jnp.zeros((128, 256), F32)
    for ref in refs:
        for a in range(4):
            wide = ref[a].astype(F32)
            total = total + wide * wide
    mean = jnp.sum(total, axis=1, keepdims=True) * (1.0 / 4096.0)
    factor = jnp.broadcast_to(lax.rsqrt(mean + 1e-05), (128, 256))
    for ref, shift in zip(refs, SHIFTS):
        near = lax.rem(place_ref[0] + 4 - shift, 4)
        for a in range(4):
            block = 4 * a + near
            gain = gain_ref[pl.ds(block, 1), :]
            normed = ref[a].astype(F32) * factor * gain
            left, right = normed[:, :128], normed[:, 128:]
            keep_ref[block] = jnp.where(first, left, right).astype(BF16)
            give_ref[block] = jnp.where(first, right, left).astype(BF16)


def norm(place, blocks, gain):
    vmem = pl.BlockSpec(memory_space=pltpu.VMEM)
    return pl.pallas_call(
        norm_kernel,
        in_specs=[pl.BlockSpec(memory_space=pltpu.SMEM)] + [vmem] * 5,
        out_specs=[vmem] * 2,
        out_shape=[jax.ShapeDtypeStruct((16, 128, 128), BF16)] * 2,
        compiler_params=PARAMS,
        name="norm",
    )(place, *blocks, gain)


def project_kernel(place_ref, keep_ref, got_ref, w_ref, out_ref):
    core = place_ref[1]
    total = [0.0, 0.0]
    for group in range(4):
        planes = range(4 * group, 4 * group + 4)
        left = jnp.concatenate(
            [
                jnp.concatenate([tokens[plane] for plane in planes], axis=1)
                for tokens in (keep_ref, got_ref)
            ],
            axis=0,
        )
        for kind in range(2):
            rows = pl.ds(128 * kind, 128)
            right = jnp.concatenate([w_ref[plane, rows, :] for plane in planes], axis=0)
            total[kind] += jnp.dot(left, right, preferred_element_type=F32)
    for side, owner in enumerate((core, 1 - core)):
        for kind in range(2):
            part = total[kind][128 * side : 128 * side + 128]
            out_ref[:, owner, pl.ds(8 * kind, 8), :] = part.T.reshape(32, 8, 128)


def project(place, keep, got, weights):
    vmem = pl.BlockSpec(memory_space=pltpu.VMEM)
    return pl.pallas_call(
        project_kernel,
        in_specs=[pl.BlockSpec(memory_space=pltpu.SMEM)] + [vmem] * 3,
        out_specs=vmem,
        out_shape=jax.ShapeDtypeStruct((32, 2, 16, 128), F32),
        compiler_params=PARAMS,
        name="project",
    )(place, keep, got, weights)


def newton_kernel(pre_ref, par_ref, out_ref, cand_ref, gate_ref):
    rec_gate, rec_cand, bias = par_ref[0:1, :], par_ref[1:2, :], par_ref[2:3, :]
    for half in range(2):
        chips = slice(8 * half, 8 * half + 8)
        for ref, rows in ((cand_ref, slice(0, 8)), (gate_ref, slice(8, 16))):
            both = pre_ref[chips, 0, :, rows, :] + pre_ref[chips, 1, :, rows, :]
            ref[half] = both.reshape(128, 128).T
    row = lax.broadcasted_iota(jnp.int32, (8, 256), 0)
    lane = lax.broadcasted_iota(jnp.int32, (8, 256), 1)

    def tokens_of(ref, r):
        picked = pl.ds(r, 8, stride=16)
        return jnp.concatenate([ref[0, picked, :], ref[1, picked, :]], axis=1)

    def shifted(a, b, by, axis):
        inside = (row if axis == 0 else lane) >= by
        return (
            jnp.where(inside, pltpu.roll(a, by, axis), 1.0),
            jnp.where(inside, pltpu.roll(b, by, axis), 0.0),
        )

    def entering(a, b):
        for by in (1, 2, 4):
            ea, eb = shifted(a, b, by, 0)
            a, b = a * ea, a * eb + b
        ta = jnp.broadcast_to(a[7:8, :], (8, 256))
        tb = jnp.broadcast_to(b[7:8, :], (8, 256))
        for by in (8, 16, 32, 64, 128):
            ea, eb = shifted(ta, tb, by, 1)
            ta, tb = ta * ea, ta * eb + tb
        carried = jnp.where(lane >= 8, pltpu.roll(tb, 8, 1), 0.0)
        ea, eb = shifted(a, b, 1, 0)
        return ea * carried + eb

    state = [jnp.zeros((8, 256), F32)] * 16
    carry = jnp.zeros((8, 256), F32)
    for _ in range(NEWTON):
        sweep = []
        for r in range(16):
            previous = carry if r == 0 else state[r - 1]
            cand_pre = tokens_of(cand_ref, r)
            gate_pre = tokens_of(gate_ref, r)
            gate = jax.nn.sigmoid(gate_pre + rec_gate * previous + bias)
            cand = jnp.tanh(cand_pre + rec_cand * previous)
            rest = 1.0 - gate
            value = gate * previous + rest * cand
            slope = (
                gate
                + gate * rest * rec_gate * (previous - cand)
                + rest * (1.0 - cand * cand) * rec_cand
            )
            offset = value - slope * previous
            if r > 0:
                slope, offset = slope * sweep[-1][0], slope * sweep[-1][1] + offset
            sweep.append((slope, offset))
        carry = entering(*sweep[-1])
        state = [a * carry + b for a, b in sweep]
    for r in range(16):
        for half in range(2):
            gate_ref[half, pl.ds(r, 8, stride=16), :] = state[r][:, 128 * half : 128 * half + 128]
    turned = jnp.concatenate([gate_ref[0].T, gate_ref[1].T], axis=0).reshape(32, 1, 8, 128)
    out_ref[...] = jnp.broadcast_to(turned, (32, 4, 8, 128)).reshape(1024, 128).astype(BF16)


def newton(pre, par):
    return pl.pallas_call(
        newton_kernel,
        out_shape=jax.ShapeDtypeStruct((1024, 128), BF16),
        scratch_shapes=[pltpu.VMEM((2, 128, 128), F32)] * 2,
        compiler_params=PARAMS,
        name="newton",
    )(pre, par)


def output_kernel(place_ref, state_ref, own_ref, mine_ref, peer_ref, out_ref, kept_ref, rows_ref):
    near, core, far = place_ref[0], place_ref[1], place_ref[2]
    wide = state_ref[...].astype(F32).reshape(32, 4, 8, 128)
    for b in range(4):
        rows_ref[b] = wide[:, b].reshape(256, 128)
    left = [rows_ref[near].T]
    for half in (core, 1 - core):
        rows = pl.ds(pl.multiple_of(half * 128, 128), 128)
        left += [rows_ref[lax.rem(near + 4 - shift, 4), rows, :].T for shift in SHIFTS[1:]]
    left = jnp.concatenate(left, axis=1).astype(BF16)
    for a in range(4):
        right = [own_ref[a]] + [ref[d, a] for ref in (mine_ref, peer_ref) for d in range(3)]
        part = jnp.dot(left, jnp.concatenate(right, axis=0), preferred_element_type=F32)
        out_ref[a] = part.astype(BF16)

        @pl.when(far == a)
        def _():
            kept_ref[...] = part


def output(place, state, own, mine, peer):
    vmem = pl.BlockSpec(memory_space=pltpu.VMEM)
    return pl.pallas_call(
        output_kernel,
        in_specs=[pl.BlockSpec(memory_space=pltpu.SMEM)] + [vmem] * 4,
        out_specs=[vmem] * 2,
        out_shape=[
            jax.ShapeDtypeStruct((4, 128, 256), BF16),
            jax.ShapeDtypeStruct((128, 256), F32),
        ],
        scratch_shapes=[pltpu.VMEM((4, 256, 128), F32)],
        compiler_params=PARAMS,
        name="output",
    )(place, state, own, mine, peer)


def total_kernel(place_ref, kept_ref, sums_ref, out_ref):
    total = kept_ref[...]
    for a in range(4):
        total = total + jnp.where(place_ref[2] == a, 0.0, sums_ref[a].astype(F32))
    out_ref[...] = total.astype(BF16)


def total(place, kept, sums):
    vmem = pl.BlockSpec(memory_space=pltpu.VMEM)
    return pl.pallas_call(
        total_kernel,
        in_specs=[pl.BlockSpec(memory_space=pltpu.SMEM), vmem, vmem],
        out_specs=vmem,
        out_shape=jax.ShapeDtypeStruct((128, 256), BF16),
        compiler_params=PARAMS,
        name="total",
    )(place, kept, sums)


def moved(array, axes, size, shift):
    return lax.ppermute(array, axes, [(i, (i + shift) % size) for i in range(size)])


def per_device(tokens, norm_gain, w_cand, w_gate, rec_gate, rec_cand, bias_gate, w_out):
    place = jnp.stack([lax.axis_index(axis) for axis in ("zb", "c", "za", "x", "y")])
    mine = lax.axis_index(SEQ)

    weights = jnp.broadcast_to(jnp.concatenate([w_cand, w_gate], axis=0), (16, 256, 256))
    far = lax.all_gather(tokens, "za", axis=0)
    weights, far = lax.optimization_barrier((weights, far))
    weights = lax.all_to_all(weights, ("x", "y"), 0, 0, tiled=True)
    own, *parts = pick(place, w_out)
    *parts, far = lax.optimization_barrier((*parts, far))
    blocks = [far] + [moved(far, ("za", "zb"), 16, shift) for shift in (1, 15, 2)]
    for i in (0, 1):
        parts[i] = moved(parts[i], "zb", 4, SHIFTS[1 + i])
    keep, give = norm(place, blocks, norm_gain.reshape(16, 256))
    give, parts[0] = lax.optimization_barrier((give, parts[0]))
    give, parts[1] = lax.optimization_barrier((give, parts[1]))
    got = lax.ppermute(give, "c", [(0, 1), (1, 0)])

    par = jnp.stack([rec_gate, rec_cand, bias_gate])
    par = jnp.tile(lax.dynamic_slice(par, (0, mine * 8), (3, 8)), (1, 32))

    pre = project(place, keep, got, weights)
    late = [parts[i] for i in (2,)]
    pre, *late = lax.optimization_barrier((pre, *late))
    for i, part in zip((2,), late):
        parts[i] = moved(part, "zb", 4, SHIFTS[1 + i])
    pre = lax.all_to_all(pre.reshape(32, 32, 128), SEQ, 0, 0, tiled=True)
    state = newton(pre.reshape(16, 2, 2, 16, 128), par)
    state, *parts = lax.optimization_barrier((state, *parts))
    half = jnp.stack(parts)
    peer = lax.ppermute(half, "c", [(0, 1), (1, 0)])
    state = lax.all_to_all(state.reshape(128, 8, 128), SEQ + ("zb",), 0, 0, tiled=True)
    sums, kept = output(place, state.reshape(1024, 128), own, half, peer)
    sums = lax.all_to_all(sums, "za", 0, 0, tiled=True)
    return total(place, kept, sums)


def solution(mesh):
    fine = Mesh(mesh.devices.reshape(4, 4, 2, 4, 4), ("x", "y", "c", "za", "zb"))
    z = ("za", "zb")
    placed = (P(SEQ, z), P(), P(SEQ, z), P(SEQ, z), P(z), P(z), P(z), P(z, None))
    return jax.shard_map(per_device, mesh=fine, in_specs=placed, out_specs=P(SEQ, z), check_vma=False)
```

```python
import jax
import jax.numpy as jnp
from jax import lax
from jax.experimental import pallas as pl
from jax.experimental.pallas import tpu as pltpu
from jax.sharding import Mesh, PartitionSpec as P

NEWTON = 3
SEQ = ("x", "y", "c")
F32 = jnp.float32
BF16 = jnp.bfloat16
PARAMS = pltpu.CompilerParams(vmem_limit_bytes=48 * 1024 * 1024)


SHIFTS = (0, 1, 3, 2)


def pick_kernel(place_ref, w_ref, own_ref, *outs):
    near, core = place_ref[0], place_ref[1]
    for a in range(4):
        columns = pl.ds(pl.multiple_of((4 * a + near) * 256, 256), 256)
        own_ref[a] = w_ref[:, columns]
    rows = pl.ds(pl.multiple_of(core * 128, 128), 128)
    for out_ref, shift in zip(outs, SHIFTS[1:]):
        for a in range(4):
            block = 4 * a + lax.rem(near + shift, 4)
            out_ref[a] = w_ref[rows, pl.ds(pl.multiple_of(block * 256, 256), 256)]


def pick(place, w_out):
    vmem = pl.BlockSpec(memory_space=pltpu.VMEM)
    shapes = [(4, 256, 256)] + [(4, 128, 256)] * 3
    return pl.pallas_call(
        pick_kernel,
        in_specs=[pl.BlockSpec(memory_space=pltpu.SMEM), vmem],
        out_specs=[vmem] * 4,
        out_shape=[jax.ShapeDtypeStruct(shape, BF16) for shape in shapes],
        compiler_params=PARAMS,
        name="pick",
    )(place, w_out)


def norm_kernel(place_ref, own_ref, up_ref, down_ref, two_ref, gain_ref, keep_ref, give_ref):
    refs = (own_ref, up_ref, down_ref, two_ref)
    first = place_ref[1] == 0
    total = jnp.zeros((128, 256), F32)
    for ref in refs:
        for a in range(4):
            wide = ref[a].astype(F32)
            total = total + wide * wide
    mean = jnp.sum(total, axis=1, keepdims=True) * (1.0 / 4096.0)
    factor = jnp.broadcast_to(lax.rsqrt(mean + 1e-05), (128, 256))
    for ref, shift in zip(refs, SHIFTS):
        near = lax.rem(place_ref[0] + 4 - shift, 4)
        for a in range(4):
            block = 4 * a + near
            gain = gain_ref[pl.ds(block, 1), :]
            normed = ref[a].astype(F32) * factor * gain
            left, right = normed[:, :128], normed[:, 128:]
            keep_ref[block] = jnp.where(first, left, right).astype(BF16)
            give_ref[block] = jnp.where(first, right, left).astype(BF16)


def norm(place, blocks, gain):
    vmem = pl.BlockSpec(memory_space=pltpu.VMEM)
    return pl.pallas_call(
        norm_kernel,
        in_specs=[pl.BlockSpec(memory_space=pltpu.SMEM)] + [vmem] * 5,
        out_specs=[vmem] * 2,
        out_shape=[jax.ShapeDtypeStruct((16, 128, 128), BF16)] * 2,
        compiler_params=PARAMS,
        name="norm",
    )(place, *blocks, gain)


def project_kernel(place_ref, keep_ref, got_ref, w_ref, out_ref):
    core = place_ref[1]
    total = [0.0, 0.0]
    for group in range(4):
        planes = range(4 * group, 4 * group + 4)
        left = jnp.concatenate(
            [
                jnp.concatenate([tokens[plane] for plane in planes], axis=1)
                for tokens in (keep_ref, got_ref)
            ],
            axis=0,
        )
        for kind in range(2):
            rows = pl.ds(128 * kind, 128)
            right = jnp.concatenate([w_ref[plane, rows, :] for plane in planes], axis=0)
            total[kind] += jnp.dot(left, right, preferred_element_type=F32)
    for side, owner in enumerate((core, 1 - core)):
        for kind in range(2):
            part = total[kind][128 * side : 128 * side + 128]
            out_ref[:, owner, pl.ds(8 * kind, 8), :] = part.T.reshape(32, 8, 128)


def project(place, keep, got, weights):
    vmem = pl.BlockSpec(memory_space=pltpu.VMEM)
    return pl.pallas_call(
        project_kernel,
        in_specs=[pl.BlockSpec(memory_space=pltpu.SMEM)] + [vmem] * 3,
        out_specs=vmem,
        out_shape=jax.ShapeDtypeStruct((32, 2, 16, 128), F32),
        compiler_params=PARAMS,
        name="project",
    )(place, keep, got, weights)


def newton_kernel(pre_ref, par_ref, out_ref, cand_ref, gate_ref):
    rec_gate, rec_cand, bias = par_ref[0:1, :], par_ref[1:2, :], par_ref[2:3, :]
    for half in range(2):
        chips = slice(8 * half, 8 * half + 8)
        for ref, rows in ((cand_ref, slice(0, 8)), (gate_ref, slice(8, 16))):
            both = pre_ref[chips, 0, :, rows, :] + pre_ref[chips, 1, :, rows, :]
            ref[half] = both.reshape(128, 128).T
    row = lax.broadcasted_iota(jnp.int32, (8, 256), 0)
    lane = lax.broadcasted_iota(jnp.int32, (8, 256), 1)

    def tokens_of(ref, r):
        picked = pl.ds(r, 8, stride=16)
        return jnp.concatenate([ref[0, picked, :], ref[1, picked, :]], axis=1)

    def shifted(a, b, by, axis):
        inside = (row if axis == 0 else lane) >= by
        return (
            jnp.where(inside, pltpu.roll(a, by, axis), 1.0),
            jnp.where(inside, pltpu.roll(b, by, axis), 0.0),
        )

    def entering(a, b):
        for by in (1, 2, 4):
            ea, eb = shifted(a, b, by, 0)
            a, b = a * ea, a * eb + b
        ta = jnp.broadcast_to(a[7:8, :], (8, 256))
        tb = jnp.broadcast_to(b[7:8, :], (8, 256))
        for by in (8, 16, 32, 64, 128):
            ea, eb = shifted(ta, tb, by, 1)
            ta, tb = ta * ea, ta * eb + tb
        carried = jnp.where(lane >= 8, pltpu.roll(tb, 8, 1), 0.0)
        ea, eb = shifted(a, b, 1, 0)
        return ea * carried + eb

    state = [jnp.zeros((8, 256), F32)] * 16
    carry = jnp.zeros((8, 256), F32)
    for _ in range(NEWTON):
        sweep = []
        for r in range(16):
            previous = carry if r == 0 else state[r - 1]
            cand_pre = tokens_of(cand_ref, r)
            gate_pre = tokens_of(gate_ref, r)
            gate = jax.nn.sigmoid(gate_pre + rec_gate * previous + bias)
            cand = jnp.tanh(cand_pre + rec_cand * previous)
            rest = 1.0 - gate
            value = gate * previous + rest * cand
            slope = (
                gate
                + gate * rest * rec_gate * (previous - cand)
                + rest * (1.0 - cand * cand) * rec_cand
            )
            offset = value - slope * previous
            if r > 0:
                slope, offset = slope * sweep[-1][0], slope * sweep[-1][1] + offset
            sweep.append((slope, offset))
        carry = entering(*sweep[-1])
        state = [a * carry + b for a, b in sweep]
    for r in range(16):
        for half in range(2):
            gate_ref[half, pl.ds(r, 8, stride=16), :] = state[r][:, 128 * half : 128 * half + 128]
    turned = jnp.concatenate([gate_ref[0].T, gate_ref[1].T], axis=0).reshape(32, 1, 8, 128)
    out_ref[...] = jnp.broadcast_to(turned, (32, 4, 8, 128)).reshape(1024, 128).astype(BF16)


def newton(pre, par):
    return pl.pallas_call(
        newton_kernel,
        out_shape=jax.ShapeDtypeStruct((1024, 128), BF16),
        scratch_shapes=[pltpu.VMEM((2, 128, 128), F32)] * 2,
        compiler_params=PARAMS,
        name="newton",
    )(pre, par)


def output_kernel(place_ref, state_ref, own_ref, mine_ref, peer_ref, out_ref, kept_ref, rows_ref):
    near, core, far = place_ref[0], place_ref[1], place_ref[2]
    wide = state_ref[...].astype(F32).reshape(32, 4, 8, 128)
    for b in range(4):
        rows_ref[b] = wide[:, b].reshape(256, 128)
    left = [rows_ref[near].T]
    for half in (core, 1 - core):
        rows = pl.ds(pl.multiple_of(half * 128, 128), 128)
        left += [rows_ref[lax.rem(near + 4 - shift, 4), rows, :].T for shift in SHIFTS[1:]]
    left = jnp.concatenate(left, axis=1).astype(BF16)
    for a in range(4):
        right = [own_ref[a]] + [ref[d, a] for ref in (mine_ref, peer_ref) for d in range(3)]
        part = jnp.dot(left, jnp.concatenate(right, axis=0), preferred_element_type=F32)
        out_ref[a] = part.astype(BF16)

        @pl.when(far == a)
        def _():
            kept_ref[...] = part


def output(place, state, own, mine, peer):
    vmem = pl.BlockSpec(memory_space=pltpu.VMEM)
    return pl.pallas_call(
        output_kernel,
        in_specs=[pl.BlockSpec(memory_space=pltpu.SMEM)] + [vmem] * 4,
        out_specs=[vmem] * 2,
        out_shape=[
            jax.ShapeDtypeStruct((4, 128, 256), BF16),
            jax.ShapeDtypeStruct((128, 256), F32),
        ],
        scratch_shapes=[pltpu.VMEM((4, 256, 128), F32)],
        compiler_params=PARAMS,
        name="output",
    )(place, state, own, mine, peer)


def total_kernel(place_ref, kept_ref, sums_ref, out_ref):
    total = kept_ref[...]
    for a in range(4):
        total = total + jnp.where(place_ref[2] == a, 0.0, sums_ref[a].astype(F32))
    out_ref[...] = total.astype(BF16)


def total(place, kept, sums):
    vmem = pl.BlockSpec(memory_space=pltpu.VMEM)
    return pl.pallas_call(
        total_kernel,
        in_specs=[pl.BlockSpec(memory_space=pltpu.SMEM), vmem, vmem],
        out_specs=vmem,
        out_shape=jax.ShapeDtypeStruct((128, 256), BF16),
        compiler_params=PARAMS,
        name="total",
    )(place, kept, sums)


def moved(array, axes, size, shift):
    return lax.ppermute(array, axes, [(i, (i + shift) % size) for i in range(size)])


def per_device(tokens, norm_gain, w_cand, w_gate, rec_gate, rec_cand, bias_gate, w_out):
    place = jnp.stack([lax.axis_index(axis) for axis in ("zb", "c", "za", "x", "y")])
    mine = lax.axis_index(SEQ)

    weights = jnp.broadcast_to(jnp.concatenate([w_cand, w_gate], axis=0), (16, 256, 256))
    far = lax.all_gather(tokens, "za", axis=0)
    weights, far = lax.optimization_barrier((weights, far))
    weights = lax.all_to_all(weights, ("x", "y"), 0, 0, tiled=True)
    own, *parts = pick(place, w_out)
    *parts, far = lax.optimization_barrier((*parts, far))
    blocks = [far] + [moved(far, ("za", "zb"), 16, shift) for shift in (1, 15, 2)]
    for i in (0, 1):
        parts[i] = moved(parts[i], "zb", 4, SHIFTS[1 + i])
    keep, give = norm(place, blocks, norm_gain.reshape(16, 256))
    give, parts[0] = lax.optimization_barrier((give, parts[0]))
    give, parts[1] = lax.optimization_barrier((give, parts[1]))
    give, weights = lax.optimization_barrier((give, weights))
    got = lax.ppermute(give, "c", [(0, 1), (1, 0)])

    par = jnp.stack([rec_gate, rec_cand, bias_gate])
    par = jnp.tile(lax.dynamic_slice(par, (0, mine * 8), (3, 8)), (1, 32))

    pre = project(place, keep, got, weights)
    late = [parts[i] for i in (2,)]
    pre, *late = lax.optimization_barrier((pre, *late))
    for i, part in zip((2,), late):
        parts[i] = moved(part, "zb", 4, SHIFTS[1 + i])
    pre = lax.all_to_all(pre.reshape(32, 32, 128), SEQ, 0, 0, tiled=True)
    state = newton(pre.reshape(16, 2, 2, 16, 128), par)
    state, *parts = lax.optimization_barrier((state, *parts))
    half = jnp.stack(parts)
    peer = lax.ppermute(half, "c", [(0, 1), (1, 0)])
    state = lax.all_to_all(state.reshape(128, 8, 128), SEQ + ("zb",), 0, 0, tiled=True)
    sums, kept = output(place, state.reshape(1024, 128), own, half, peer)
    sums = lax.all_to_all(sums, "za", 0, 0, tiled=True)
    return total(place, kept, sums)


def solution(mesh):
    fine = Mesh(mesh.devices.reshape(4, 4, 2, 4, 4), ("x", "y", "c", "za", "zb"))
    z = ("za", "zb")
    placed = (P(SEQ, z), P(), P(SEQ, z), P(SEQ, z), P(z), P(z), P(z), P(z, None))
    return jax.shard_map(per_device, mesh=fine, in_specs=placed, out_specs=P(SEQ, z), check_vma=False)
```

```python
import jax
import jax.numpy as jnp
from jax import lax
from jax.experimental import pallas as pl
from jax.experimental.pallas import tpu as pltpu
from jax.sharding import Mesh, PartitionSpec as P

NEWTON = 3
SEQ = ("x", "y", "c")
F32 = jnp.float32
BF16 = jnp.bfloat16
PARAMS = pltpu.CompilerParams(vmem_limit_bytes=48 * 1024 * 1024)


SHIFTS = (0, 1, 3, 2)


def pick_kernel(place_ref, w_ref, own_ref, *outs):
    near, core = place_ref[0], place_ref[1]
    for a in range(4):
        columns = pl.ds(pl.multiple_of((4 * a + near) * 256, 256), 256)
        own_ref[a] = w_ref[:, columns]
    rows = pl.ds(pl.multiple_of(core * 128, 128), 128)
    for out_ref, shift in zip(outs, SHIFTS[1:]):
        for a in range(4):
            block = 4 * a + lax.rem(near + shift, 4)
            out_ref[a] = w_ref[rows, pl.ds(pl.multiple_of(block * 256, 256), 256)]


def pick(place, w_out):
    vmem = pl.BlockSpec(memory_space=pltpu.VMEM)
    shapes = [(4, 256, 256)] + [(4, 128, 256)] * 3
    return pl.pallas_call(
        pick_kernel,
        in_specs=[pl.BlockSpec(memory_space=pltpu.SMEM), vmem],
        out_specs=[vmem] * 4,
        out_shape=[jax.ShapeDtypeStruct(shape, BF16) for shape in shapes],
        compiler_params=PARAMS,
        name="pick",
    )(place, w_out)


def norm_kernel(place_ref, own_ref, up_ref, down_ref, two_ref, gain_ref, keep_ref, give_ref):
    refs = (own_ref, up_ref, down_ref, two_ref)
    first = place_ref[1] == 0
    total = jnp.zeros((128, 256), F32)
    for ref in refs:
        for a in range(4):
            wide = ref[a].astype(F32)
            total = total + wide * wide
    mean = jnp.sum(total, axis=1, keepdims=True) * (1.0 / 4096.0)
    factor = jnp.broadcast_to(lax.rsqrt(mean + 1e-05), (128, 256))
    for ref, shift in zip(refs, SHIFTS):
        near = lax.rem(place_ref[0] + 4 - shift, 4)
        for a in range(4):
            block = 4 * a + near
            gain = gain_ref[pl.ds(block, 1), :]
            normed = ref[a].astype(F32) * factor * gain
            left, right = normed[:, :128], normed[:, 128:]
            keep_ref[block] = jnp.where(first, left, right).astype(BF16)
            give_ref[block] = jnp.where(first, right, left).astype(BF16)


def norm(place, blocks, gain):
    vmem = pl.BlockSpec(memory_space=pltpu.VMEM)
    return pl.pallas_call(
        norm_kernel,
        in_specs=[pl.BlockSpec(memory_space=pltpu.SMEM)] + [vmem] * 5,
        out_specs=[vmem] * 2,
        out_shape=[jax.ShapeDtypeStruct((16, 128, 128), BF16)] * 2,
        compiler_params=PARAMS,
        name="norm",
    )(place, *blocks, gain)


def project_kernel(place_ref, keep_ref, got_ref, w_ref, out_ref):
    core = place_ref[1]
    total = [0.0, 0.0]
    for group in range(4):
        planes = range(4 * group, 4 * group + 4)
        left = jnp.concatenate(
            [
                jnp.concatenate([tokens[plane] for plane in planes], axis=1)
                for tokens in (keep_ref, got_ref)
            ],
            axis=0,
        )
        for kind in range(2):
            rows = pl.ds(128 * kind, 128)
            right = jnp.concatenate([w_ref[plane, rows, :] for plane in planes], axis=0)
            total[kind] += jnp.dot(left, right, preferred_element_type=F32)
    for side, owner in enumerate((core, 1 - core)):
        for kind in range(2):
            part = total[kind][128 * side : 128 * side + 128]
            out_ref[:, owner, pl.ds(8 * kind, 8), :] = part.T.reshape(32, 8, 128)


def project(place, keep, got, weights):
    vmem = pl.BlockSpec(memory_space=pltpu.VMEM)
    return pl.pallas_call(
        project_kernel,
        in_specs=[pl.BlockSpec(memory_space=pltpu.SMEM)] + [vmem] * 3,
        out_specs=vmem,
        out_shape=jax.ShapeDtypeStruct((32, 2, 16, 128), F32),
        compiler_params=PARAMS,
        name="project",
    )(place, keep, got, weights)


def newton_kernel(pre_ref, par_ref, out_ref, cand_ref, gate_ref):
    rec_gate, rec_cand, bias = par_ref[0:1, :], par_ref[1:2, :], par_ref[2:3, :]
    for half in range(2):
        chips = slice(8 * half, 8 * half + 8)
        for ref, rows in ((cand_ref, slice(0, 8)), (gate_ref, slice(8, 16))):
            both = pre_ref[chips, 0, :, rows, :] + pre_ref[chips, 1, :, rows, :]
            ref[half] = both.reshape(128, 128).T
    row = lax.broadcasted_iota(jnp.int32, (8, 256), 0)
    lane = lax.broadcasted_iota(jnp.int32, (8, 256), 1)

    def tokens_of(ref, r):
        picked = pl.ds(r, 8, stride=16)
        return jnp.concatenate([ref[0, picked, :], ref[1, picked, :]], axis=1)

    def shifted(a, b, by, axis):
        inside = (row if axis == 0 else lane) >= by
        return (
            jnp.where(inside, pltpu.roll(a, by, axis), 1.0),
            jnp.where(inside, pltpu.roll(b, by, axis), 0.0),
        )

    def entering(a, b):
        for by in (1, 2, 4):
            ea, eb = shifted(a, b, by, 0)
            a, b = a * ea, a * eb + b
        ta = jnp.broadcast_to(a[7:8, :], (8, 256))
        tb = jnp.broadcast_to(b[7:8, :], (8, 256))
        for by in (8, 16, 32, 64, 128):
            ea, eb = shifted(ta, tb, by, 1)
            ta, tb = ta * ea, ta * eb + tb
        carried = jnp.where(lane >= 8, pltpu.roll(tb, 8, 1), 0.0)
        ea, eb = shifted(a, b, 1, 0)
        return ea * carried + eb

    state = [jnp.zeros((8, 256), F32)] * 16
    carry = jnp.zeros((8, 256), F32)
    for _ in range(NEWTON):
        sweep = []
        for r in range(16):
            previous = carry if r == 0 else state[r - 1]
            cand_pre = tokens_of(cand_ref, r)
            gate_pre = tokens_of(gate_ref, r)
            gate = jax.nn.sigmoid(gate_pre + rec_gate * previous + bias)
            cand = jnp.tanh(cand_pre + rec_cand * previous)
            rest = 1.0 - gate
            value = gate * previous + rest * cand
            slope = (
                gate
                + gate * rest * rec_gate * (previous - cand)
                + rest * (1.0 - cand * cand) * rec_cand
            )
            offset = value - slope * previous
            if r > 0:
                slope, offset = slope * sweep[-1][0], slope * sweep[-1][1] + offset
            sweep.append((slope, offset))
        carry = entering(*sweep[-1])
        state = [a * carry + b for a, b in sweep]
    for r in range(16):
        for half in range(2):
            gate_ref[half, pl.ds(r, 8, stride=16), :] = state[r][:, 128 * half : 128 * half + 128]
    turned = jnp.concatenate([gate_ref[0].T, gate_ref[1].T], axis=0).reshape(32, 1, 8, 128)
    out_ref[...] = jnp.broadcast_to(turned, (32, 4, 8, 128)).reshape(1024, 128).astype(BF16)


def newton(pre, par):
    return pl.pallas_call(
        newton_kernel,
        out_shape=jax.ShapeDtypeStruct((1024, 128), BF16),
        scratch_shapes=[pltpu.VMEM((2, 128, 128), F32)] * 2,
        compiler_params=PARAMS,
        name="newton",
    )(pre, par)


def output_kernel(place_ref, state_ref, own_ref, mine_ref, peer_ref, out_ref, kept_ref, rows_ref):
    near, core, far = place_ref[0], place_ref[1], place_ref[2]
    wide = state_ref[...].astype(F32).reshape(32, 4, 8, 128)
    for b in range(4):
        rows_ref[b] = wide[:, b].reshape(256, 128)
    left = [rows_ref[near].T]
    for half in (core, 1 - core):
        rows = pl.ds(pl.multiple_of(half * 128, 128), 128)
        left += [rows_ref[lax.rem(near + 4 - shift, 4), rows, :].T for shift in SHIFTS[1:]]
    left = jnp.concatenate(left, axis=1).astype(BF16)
    for a in range(4):
        right = [own_ref[a]] + [ref[d, a] for ref in (mine_ref, peer_ref) for d in range(3)]
        part = jnp.dot(left, jnp.concatenate(right, axis=0), preferred_element_type=F32)
        out_ref[a] = part.astype(BF16)

        @pl.when(far == a)
        def _():
            kept_ref[...] = part


def output(place, state, own, mine, peer):
    vmem = pl.BlockSpec(memory_space=pltpu.VMEM)
    return pl.pallas_call(
        output_kernel,
        in_specs=[pl.BlockSpec(memory_space=pltpu.SMEM)] + [vmem] * 4,
        out_specs=[vmem] * 2,
        out_shape=[
            jax.ShapeDtypeStruct((4, 128, 256), BF16),
            jax.ShapeDtypeStruct((128, 256), F32),
        ],
        scratch_shapes=[pltpu.VMEM((4, 256, 128), F32)],
        compiler_params=PARAMS,
        name="output",
    )(place, state, own, mine, peer)


def total_kernel(place_ref, kept_ref, sums_ref, out_ref):
    total = kept_ref[...]
    for a in range(4):
        total = total + jnp.where(place_ref[2] == a, 0.0, sums_ref[a].astype(F32))
    out_ref[...] = total.astype(BF16)


def total(place, kept, sums):
    vmem = pl.BlockSpec(memory_space=pltpu.VMEM)
    return pl.pallas_call(
        total_kernel,
        in_specs=[pl.BlockSpec(memory_space=pltpu.SMEM), vmem, vmem],
        out_specs=vmem,
        out_shape=jax.ShapeDtypeStruct((128, 256), BF16),
        compiler_params=PARAMS,
        name="total",
    )(place, kept, sums)


def moved(array, axes, size, shift):
    return lax.ppermute(array, axes, [(i, (i + shift) % size) for i in range(size)])


def per_device(tokens, norm_gain, w_cand, w_gate, rec_gate, rec_cand, bias_gate, w_out):
    place = jnp.stack([lax.axis_index(axis) for axis in ("zb", "c", "za", "x", "y")])
    mine = lax.axis_index(SEQ)

    weights = jnp.broadcast_to(jnp.concatenate([w_cand, w_gate], axis=0), (16, 256, 256))
    far = lax.all_gather(tokens, "za", axis=0)
    weights, far = lax.optimization_barrier((weights, far))
    weights = lax.all_to_all(weights, ("x", "y"), 0, 0, tiled=True)
    own, *parts = pick(place, w_out)
    *parts, far = lax.optimization_barrier((*parts, far))
    blocks = [far] + [moved(far, ("za", "zb"), 16, shift) for shift in (1, 15, 2)]
    for i in (0,):
        parts[i] = moved(parts[i], "zb", 4, SHIFTS[1 + i])
    keep, give = norm(place, blocks, norm_gain.reshape(16, 256))
    give, parts[0] = lax.optimization_barrier((give, parts[0]))
    give, weights = lax.optimization_barrier((give, weights))
    got = lax.ppermute(give, "c", [(0, 1), (1, 0)])

    par = jnp.stack([rec_gate, rec_cand, bias_gate])
    par = jnp.tile(lax.dynamic_slice(par, (0, mine * 8), (3, 8)), (1, 32))

    pre = project(place, keep, got, weights)
    late = [parts[i] for i in (2, 1)]
    pre, *late = lax.optimization_barrier((pre, *late))
    for i, part in zip((2, 1), late):
        parts[i] = moved(part, "zb", 4, SHIFTS[1 + i])
    pre = lax.all_to_all(pre.reshape(32, 32, 128), SEQ, 0, 0, tiled=True)
    state = newton(pre.reshape(16, 2, 2, 16, 128), par)
    half = jnp.stack(parts)
    peer = lax.ppermute(half, "c", [(0, 1), (1, 0)])
    state = lax.all_to_all(state.reshape(128, 8, 128), SEQ + ("zb",), 0, 0, tiled=True)
    sums, kept = output(place, state.reshape(1024, 128), own, half, peer)
    sums = lax.all_to_all(sums, "za", 0, 0, tiled=True)
    return total(place, kept, sums)


def solution(mesh):
    fine = Mesh(mesh.devices.reshape(4, 4, 2, 4, 4), ("x", "y", "c", "za", "zb"))
    z = ("za", "zb")
    placed = (P(SEQ, z), P(), P(SEQ, z), P(SEQ, z), P(z), P(z), P(z), P(z, None))
    return jax.shard_map(per_device, mesh=fine, in_specs=placed, out_specs=P(SEQ, z), check_vma=False)
```

```python
import jax
import jax.numpy as jnp
from jax import lax
from jax.experimental import pallas as pl
from jax.experimental.pallas import tpu as pltpu
from jax.sharding import Mesh, PartitionSpec as P

NEWTON = 3
SEQ = ("x", "y", "c")
F32 = jnp.float32
BF16 = jnp.bfloat16
PARAMS = pltpu.CompilerParams(vmem_limit_bytes=48 * 1024 * 1024)


SHIFTS = (0, 2, 1, 3)


def pick_kernel(place_ref, w_ref, own_ref, *outs):
    near, core = place_ref[0], place_ref[1]
    for a in range(4):
        columns = pl.ds(pl.multiple_of((4 * a + near) * 256, 256), 256)
        own_ref[a] = w_ref[:, columns]
    rows = pl.ds(pl.multiple_of(core * 128, 128), 128)
    for out_ref, shift in zip(outs, SHIFTS[1:]):
        for a in range(4):
            block = 4 * a + lax.rem(near + shift, 4)
            out_ref[a] = w_ref[rows, pl.ds(pl.multiple_of(block * 256, 256), 256)]


def pick(place, w_out):
    vmem = pl.BlockSpec(memory_space=pltpu.VMEM)
    shapes = [(4, 256, 256)] + [(4, 128, 256)] * 3
    return pl.pallas_call(
        pick_kernel,
        in_specs=[pl.BlockSpec(memory_space=pltpu.SMEM), vmem],
        out_specs=[vmem] * 4,
        out_shape=[jax.ShapeDtypeStruct(shape, BF16) for shape in shapes],
        compiler_params=PARAMS,
        name="pick",
    )(place, w_out)


def norm_kernel(place_ref, own_ref, two_ref, up_ref, down_ref, gain_ref, keep_ref, give_ref):
    refs = (own_ref, two_ref, up_ref, down_ref)
    first = place_ref[1] == 0
    total = jnp.zeros((128, 256), F32)
    for ref in refs:
        for a in range(4):
            wide = ref[a].astype(F32)
            total = total + wide * wide
    mean = jnp.sum(total, axis=1, keepdims=True) * (1.0 / 4096.0)
    factor = jnp.broadcast_to(lax.rsqrt(mean + 1e-05), (128, 256))
    for ref, shift in zip(refs, SHIFTS):
        near = lax.rem(place_ref[0] + 4 - shift, 4)
        for a in range(4):
            block = 4 * a + near
            gain = gain_ref[pl.ds(block, 1), :]
            normed = ref[a].astype(F32) * factor * gain
            left, right = normed[:, :128], normed[:, 128:]
            keep_ref[block] = jnp.where(first, left, right).astype(BF16)
            give_ref[block] = jnp.where(first, right, left).astype(BF16)


def norm(place, blocks, gain):
    vmem = pl.BlockSpec(memory_space=pltpu.VMEM)
    return pl.pallas_call(
        norm_kernel,
        in_specs=[pl.BlockSpec(memory_space=pltpu.SMEM)] + [vmem] * 5,
        out_specs=[vmem] * 2,
        out_shape=[jax.ShapeDtypeStruct((16, 128, 128), BF16)] * 2,
        compiler_params=PARAMS,
        name="norm",
    )(place, *blocks, gain)


def project_kernel(place_ref, keep_ref, got_ref, w_ref, out_ref):
    core = place_ref[1]
    total = [0.0, 0.0]
    for group in range(4):
        planes = range(4 * group, 4 * group + 4)
        left = jnp.concatenate(
            [
                jnp.concatenate([tokens[plane] for plane in planes], axis=1)
                for tokens in (keep_ref, got_ref)
            ],
            axis=0,
        )
        for kind in range(2):
            rows = pl.ds(128 * kind, 128)
            right = jnp.concatenate([w_ref[plane, rows, :] for plane in planes], axis=0)
            total[kind] += jnp.dot(left, right, preferred_element_type=F32)
    for side, owner in enumerate((core, 1 - core)):
        for kind in range(2):
            part = total[kind][128 * side : 128 * side + 128]
            out_ref[:, owner, pl.ds(8 * kind, 8), :] = part.T.reshape(32, 8, 128)


def project(place, keep, got, weights):
    vmem = pl.BlockSpec(memory_space=pltpu.VMEM)
    return pl.pallas_call(
        project_kernel,
        in_specs=[pl.BlockSpec(memory_space=pltpu.SMEM)] + [vmem] * 3,
        out_specs=vmem,
        out_shape=jax.ShapeDtypeStruct((32, 2, 16, 128), F32),
        compiler_params=PARAMS,
        name="project",
    )(place, keep, got, weights)


def newton_kernel(pre_ref, par_ref, out_ref, cand_ref, gate_ref):
    rec_gate, rec_cand, bias = par_ref[0:1, :], par_ref[1:2, :], par_ref[2:3, :]
    for half in range(2):
        chips = slice(8 * half, 8 * half + 8)
        for ref, rows in ((cand_ref, slice(0, 8)), (gate_ref, slice(8, 16))):
            both = pre_ref[chips, 0, :, rows, :] + pre_ref[chips, 1, :, rows, :]
            ref[half] = both.reshape(128, 128).T
    row = lax.broadcasted_iota(jnp.int32, (8, 256), 0)
    lane = lax.broadcasted_iota(jnp.int32, (8, 256), 1)

    def tokens_of(ref, r):
        picked = pl.ds(r, 8, stride=16)
        return jnp.concatenate([ref[0, picked, :], ref[1, picked, :]], axis=1)

    def shifted(a, b, by, axis):
        inside = (row if axis == 0 else lane) >= by
        return (
            jnp.where(inside, pltpu.roll(a, by, axis), 1.0),
            jnp.where(inside, pltpu.roll(b, by, axis), 0.0),
        )

    def entering(a, b):
        for by in (1, 2, 4):
            ea, eb = shifted(a, b, by, 0)
            a, b = a * ea, a * eb + b
        ta = jnp.broadcast_to(a[7:8, :], (8, 256))
        tb = jnp.broadcast_to(b[7:8, :], (8, 256))
        for by in (8, 16, 32, 64, 128):
            ea, eb = shifted(ta, tb, by, 1)
            ta, tb = ta * ea, ta * eb + tb
        carried = jnp.where(lane >= 8, pltpu.roll(tb, 8, 1), 0.0)
        ea, eb = shifted(a, b, 1, 0)
        return ea * carried + eb

    state = [jnp.zeros((8, 256), F32)] * 16
    carry = jnp.zeros((8, 256), F32)
    for _ in range(NEWTON):
        sweep = []
        for r in range(16):
            previous = carry if r == 0 else state[r - 1]
            cand_pre = tokens_of(cand_ref, r)
            gate_pre = tokens_of(gate_ref, r)
            gate = jax.nn.sigmoid(gate_pre + rec_gate * previous + bias)
            cand = jnp.tanh(cand_pre + rec_cand * previous)
            rest = 1.0 - gate
            value = gate * previous + rest * cand
            slope = (
                gate
                + gate * rest * rec_gate * (previous - cand)
                + rest * (1.0 - cand * cand) * rec_cand
            )
            offset = value - slope * previous
            if r > 0:
                slope, offset = slope * sweep[-1][0], slope * sweep[-1][1] + offset
            sweep.append((slope, offset))
        carry = entering(*sweep[-1])
        state = [a * carry + b for a, b in sweep]
    for r in range(16):
        for half in range(2):
            gate_ref[half, pl.ds(r, 8, stride=16), :] = state[r][:, 128 * half : 128 * half + 128]
    turned = jnp.concatenate([gate_ref[0].T, gate_ref[1].T], axis=0).reshape(32, 1, 8, 128)
    out_ref[...] = jnp.broadcast_to(turned, (32, 4, 8, 128)).reshape(1024, 128).astype(BF16)


def newton(pre, par):
    return pl.pallas_call(
        newton_kernel,
        out_shape=jax.ShapeDtypeStruct((1024, 128), BF16),
        scratch_shapes=[pltpu.VMEM((2, 128, 128), F32)] * 2,
        compiler_params=PARAMS,
        name="newton",
    )(pre, par)


def output_kernel(place_ref, state_ref, own_ref, mine_ref, peer_ref, out_ref, kept_ref, rows_ref):
    near, core, far = place_ref[0], place_ref[1], place_ref[2]
    wide = state_ref[...].astype(F32).reshape(32, 4, 8, 128)
    for b in range(4):
        rows_ref[b] = wide[:, b].reshape(256, 128)
    left = [rows_ref[near].T]
    for half in (core, 1 - core):
        rows = pl.ds(pl.multiple_of(half * 128, 128), 128)
        left += [rows_ref[lax.rem(near + 4 - shift, 4), rows, :].T for shift in SHIFTS[1:]]
    left = jnp.concatenate(left, axis=1).astype(BF16)
    for a in range(4):
        right = [own_ref[a]] + [ref[d, a] for ref in (mine_ref, peer_ref) for d in range(3)]
        part = jnp.dot(left, jnp.concatenate(right, axis=0), preferred_element_type=F32)
        out_ref[a] = part.astype(BF16)

        @pl.when(far == a)
        def _():
            kept_ref[...] = part


def output(place, state, own, mine, peer):
    vmem = pl.BlockSpec(memory_space=pltpu.VMEM)
    return pl.pallas_call(
        output_kernel,
        in_specs=[pl.BlockSpec(memory_space=pltpu.SMEM)] + [vmem] * 4,
        out_specs=[vmem] * 2,
        out_shape=[
            jax.ShapeDtypeStruct((4, 128, 256), BF16),
            jax.ShapeDtypeStruct((128, 256), F32),
        ],
        scratch_shapes=[pltpu.VMEM((4, 256, 128), F32)],
        compiler_params=PARAMS,
        name="output",
    )(place, state, own, mine, peer)


def moved(array, axes, size, shift):
    return lax.ppermute(array, axes, [(i, (i + shift) % size) for i in range(size)])


def per_device(tokens, norm_gain, w_cand, w_gate, rec_gate, rec_cand, bias_gate, w_out):
    place = jnp.stack([lax.axis_index(axis) for axis in ("zb", "c", "za", "x", "y")])
    mine = lax.axis_index(SEQ)

    weights = jnp.broadcast_to(jnp.concatenate([w_cand, w_gate], axis=0), (16, 256, 256))
    far = lax.all_gather(tokens, "za", axis=0)
    weights, far = lax.optimization_barrier((weights, far))
    weights = lax.all_to_all(weights, ("x", "y"), 0, 0, tiled=True)
    blocks = [far] + [moved(far, ("za", "zb"), 16, shift) for shift in (2, 1, 15)]
    own, *parts = pick(place, w_out)
    keep, give = norm(place, blocks, norm_gain.reshape(16, 256))
    got = lax.ppermute(give, "c", [(0, 1), (1, 0)])

    par = jnp.stack([rec_gate, rec_cand, bias_gate])
    par = jnp.tile(lax.dynamic_slice(par, (0, mine * 8), (3, 8)), (1, 32))

    pre = project(place, keep, got, weights)
    pre, *parts = lax.optimization_barrier((pre, *parts))
    parts = [moved(part, "zb", 4, shift) for part, shift in zip(parts, SHIFTS[1:])]
    pre = lax.all_to_all(pre.reshape(32, 32, 128), SEQ, 0, 0, tiled=True)
    state = newton(pre.reshape(16, 2, 2, 16, 128), par)
    half = jnp.stack(parts)
    peer = lax.ppermute(half, "c", [(0, 1), (1, 0)])
    state = lax.all_to_all(state.reshape(128, 8, 128), SEQ + ("zb",), 0, 0, tiled=True)
    sums, kept = output(place, state.reshape(1024, 128), own, half, peer)
    sums = lax.all_to_all(sums, "za", 0, 0, tiled=True)
    others = jnp.arange(4)[:, None, None] != lax.axis_index("za")
    total = kept + jnp.sum(jnp.where(others, sums.astype(F32), 0.0), axis=0)
    return total.astype(BF16)


def solution(mesh):
    fine = Mesh(mesh.devices.reshape(4, 4, 2, 4, 4), ("x", "y", "c", "za", "zb"))
    z = ("za", "zb")
    placed = (P(SEQ, z), P(), P(SEQ, z), P(SEQ, z), P(z), P(z), P(z), P(z, None))
    return jax.shard_map(per_device, mesh=fine, in_specs=placed, out_specs=P(SEQ, z), check_vma=False)
```

```python
import jax
import jax.numpy as jnp
from jax import lax
from jax.experimental import pallas as pl
from jax.experimental.pallas import tpu as pltpu
from jax.sharding import Mesh, PartitionSpec as P

NEWTON = 3
SEQ = ("x", "y", "c")
F32 = jnp.float32
BF16 = jnp.bfloat16
PARAMS = pltpu.CompilerParams(vmem_limit_bytes=48 * 1024 * 1024)


SHIFTS = (0, 2, 1, 3)


def pick_kernel(place_ref, w_ref, own_ref, *outs):
    near, core = place_ref[0], place_ref[1]
    for a in range(4):
        columns = pl.ds(pl.multiple_of((4 * a + near) * 256, 256), 256)
        own_ref[a] = w_ref[:, columns]
    rows = pl.ds(pl.multiple_of(core * 128, 128), 128)
    for out_ref, shift in zip(outs, SHIFTS[1:]):
        for a in range(4):
            block = 4 * a + lax.rem(near + shift, 4)
            out_ref[a] = w_ref[rows, pl.ds(pl.multiple_of(block * 256, 256), 256)]


def pick(place, w_out):
    vmem = pl.BlockSpec(memory_space=pltpu.VMEM)
    shapes = [(4, 256, 256)] + [(4, 128, 256)] * 3
    return pl.pallas_call(
        pick_kernel,
        in_specs=[pl.BlockSpec(memory_space=pltpu.SMEM), vmem],
        out_specs=[vmem] * 4,
        out_shape=[jax.ShapeDtypeStruct(shape, BF16) for shape in shapes],
        compiler_params=PARAMS,
        name="pick",
    )(place, w_out)


def norm_kernel(place_ref, own_ref, two_ref, up_ref, down_ref, gain_ref, keep_ref, give_ref):
    refs = (own_ref, two_ref, up_ref, down_ref)
    first = place_ref[1] == 0
    total = jnp.zeros((128, 256), F32)
    for ref in refs:
        for a in range(4):
            wide = ref[a].astype(F32)
            total = total + wide * wide
    mean = jnp.sum(total, axis=1, keepdims=True) * (1.0 / 4096.0)
    factor = jnp.broadcast_to(lax.rsqrt(mean + 1e-05), (128, 256))
    for ref, shift in zip(refs, SHIFTS):
        near = lax.rem(place_ref[0] + 4 - shift, 4)
        for a in range(4):
            block = 4 * a + near
            gain = gain_ref[pl.ds(block, 1), :]
            normed = ref[a].astype(F32) * factor * gain
            left, right = normed[:, :128], normed[:, 128:]
            keep_ref[block] = jnp.where(first, left, right).astype(BF16)
            give_ref[block] = jnp.where(first, right, left).astype(BF16)


def norm(place, blocks, gain):
    vmem = pl.BlockSpec(memory_space=pltpu.VMEM)
    return pl.pallas_call(
        norm_kernel,
        in_specs=[pl.BlockSpec(memory_space=pltpu.SMEM)] + [vmem] * 5,
        out_specs=[vmem] * 2,
        out_shape=[jax.ShapeDtypeStruct((16, 128, 128), BF16)] * 2,
        compiler_params=PARAMS,
        name="norm",
    )(place, *blocks, gain)


def project_kernel(place_ref, keep_ref, got_ref, w_ref, out_ref):
    core = place_ref[1]
    total = [0.0, 0.0]
    for group in range(4):
        planes = range(4 * group, 4 * group + 4)
        left = jnp.concatenate(
            [
                jnp.concatenate([tokens[plane] for plane in planes], axis=1)
                for tokens in (keep_ref, got_ref)
            ],
            axis=0,
        )
        for kind in range(2):
            rows = pl.ds(128 * kind, 128)
            right = jnp.concatenate([w_ref[plane, rows, :] for plane in planes], axis=0)
            total[kind] += jnp.dot(left, right, preferred_element_type=F32)
    for side, owner in enumerate((core, 1 - core)):
        for kind in range(2):
            part = total[kind][128 * side : 128 * side + 128]
            out_ref[:, owner, pl.ds(8 * kind, 8), :] = part.T.reshape(32, 8, 128)


def project(place, keep, got, weights):
    vmem = pl.BlockSpec(memory_space=pltpu.VMEM)
    return pl.pallas_call(
        project_kernel,
        in_specs=[pl.BlockSpec(memory_space=pltpu.SMEM)] + [vmem] * 3,
        out_specs=vmem,
        out_shape=jax.ShapeDtypeStruct((32, 2, 16, 128), F32),
        compiler_params=PARAMS,
        name="project",
    )(place, keep, got, weights)


def newton_kernel(pre_ref, par_ref, out_ref, cand_ref, gate_ref):
    rec_gate, rec_cand, bias = par_ref[0:1, :], par_ref[1:2, :], par_ref[2:3, :]
    for half in range(2):
        chips = slice(8 * half, 8 * half + 8)
        for ref, rows in ((cand_ref, slice(0, 8)), (gate_ref, slice(8, 16))):
            both = pre_ref[chips, 0, :, rows, :] + pre_ref[chips, 1, :, rows, :]
            ref[half] = both.reshape(128, 128).T
    row = lax.broadcasted_iota(jnp.int32, (8, 256), 0)
    lane = lax.broadcasted_iota(jnp.int32, (8, 256), 1)

    def tokens_of(ref, r):
        picked = pl.ds(r, 8, stride=16)
        return jnp.concatenate([ref[0, picked, :], ref[1, picked, :]], axis=1)

    def shifted(a, b, by, axis):
        inside = (row if axis == 0 else lane) >= by
        return (
            jnp.where(inside, pltpu.roll(a, by, axis), 1.0),
            jnp.where(inside, pltpu.roll(b, by, axis), 0.0),
        )

    def entering(a, b):
        for by in (1, 2, 4):
            ea, eb = shifted(a, b, by, 0)
            a, b = a * ea, a * eb + b
        ta = jnp.broadcast_to(a[7:8, :], (8, 256))
        tb = jnp.broadcast_to(b[7:8, :], (8, 256))
        for by in (8, 16, 32, 64, 128):
            ea, eb = shifted(ta, tb, by, 1)
            ta, tb = ta * ea, ta * eb + tb
        carried = jnp.where(lane >= 8, pltpu.roll(tb, 8, 1), 0.0)
        ea, eb = shifted(a, b, 1, 0)
        return ea * carried + eb

    state = [jnp.zeros((8, 256), F32)] * 16
    carry = jnp.zeros((8, 256), F32)
    for _ in range(NEWTON):
        sweep = []
        for r in range(16):
            previous = carry if r == 0 else state[r - 1]
            cand_pre = tokens_of(cand_ref, r)
            gate_pre = tokens_of(gate_ref, r)
            gate = jax.nn.sigmoid(gate_pre + rec_gate * previous + bias)
            cand = jnp.tanh(cand_pre + rec_cand * previous)
            rest = 1.0 - gate
            value = gate * previous + rest * cand
            slope = (
                gate
                + gate * rest * rec_gate * (previous - cand)
                + rest * (1.0 - cand * cand) * rec_cand
            )
            offset = value - slope * previous
            if r > 0:
                slope, offset = slope * sweep[-1][0], slope * sweep[-1][1] + offset
            sweep.append((slope, offset))
        carry = entering(*sweep[-1])
        state = [a * carry + b for a, b in sweep]
    for r in range(16):
        for half in range(2):
            gate_ref[half, pl.ds(r, 8, stride=16), :] = state[r][:, 128 * half : 128 * half + 128]
    turned = jnp.concatenate([gate_ref[0].T, gate_ref[1].T], axis=0).reshape(32, 1, 8, 128)
    out_ref[...] = jnp.broadcast_to(turned, (32, 4, 8, 128)).reshape(1024, 128).astype(BF16)


def newton(pre, par):
    return pl.pallas_call(
        newton_kernel,
        out_shape=jax.ShapeDtypeStruct((1024, 128), BF16),
        scratch_shapes=[pltpu.VMEM((2, 128, 128), F32)] * 2,
        compiler_params=PARAMS,
        name="newton",
    )(pre, par)


def output_kernel(place_ref, state_ref, own_ref, mine_ref, peer_ref, out_ref, kept_ref, rows_ref):
    near, core, far = place_ref[0], place_ref[1], place_ref[2]
    wide = state_ref[...].astype(F32).reshape(32, 4, 8, 128)
    for b in range(4):
        rows_ref[b] = wide[:, b].reshape(256, 128)
    left = [rows_ref[near].T]
    for half in (core, 1 - core):
        rows = pl.ds(pl.multiple_of(half * 128, 128), 128)
        left += [rows_ref[lax.rem(near + 4 - shift, 4), rows, :].T for shift in SHIFTS[1:]]
    left = jnp.concatenate(left, axis=1).astype(BF16)
    for a in range(4):
        right = [own_ref[a]] + [ref[d, a] for ref in (mine_ref, peer_ref) for d in range(3)]
        part = jnp.dot(left, jnp.concatenate(right, axis=0), preferred_element_type=F32)
        out_ref[a] = part.astype(BF16)

        @pl.when(far == a)
        def _():
            kept_ref[...] = part


def output(place, state, own, mine, peer):
    vmem = pl.BlockSpec(memory_space=pltpu.VMEM)
    return pl.pallas_call(
        output_kernel,
        in_specs=[pl.BlockSpec(memory_space=pltpu.SMEM)] + [vmem] * 4,
        out_specs=[vmem] * 2,
        out_shape=[
            jax.ShapeDtypeStruct((4, 128, 256), BF16),
            jax.ShapeDtypeStruct((128, 256), F32),
        ],
        scratch_shapes=[pltpu.VMEM((4, 256, 128), F32)],
        compiler_params=PARAMS,
        name="output",
    )(place, state, own, mine, peer)


def moved(array, axes, size, shift):
    return lax.ppermute(array, axes, [(i, (i + shift) % size) for i in range(size)])


def per_device(tokens, norm_gain, w_cand, w_gate, rec_gate, rec_cand, bias_gate, w_out):
    place = jnp.stack([lax.axis_index(axis) for axis in ("zb", "c", "za", "x", "y")])
    mine = lax.axis_index(SEQ)

    weights = jnp.broadcast_to(jnp.concatenate([w_cand, w_gate], axis=0), (16, 256, 256))
    far = lax.all_gather(tokens, "za", axis=0)
    weights, far = lax.optimization_barrier((weights, far))
    weights = lax.all_to_all(weights, ("x", "y"), 0, 0, tiled=True)
    own, *parts = pick(place, w_out)
    *parts, far = lax.optimization_barrier((*parts, far))
    blocks = [far] + [moved(far, ("za", "zb"), 16, shift) for shift in (2, 1, 15)]
    for i in (1,):
        parts[i] = moved(parts[i], "zb", 4, SHIFTS[1 + i])
    keep, give = norm(place, blocks, norm_gain.reshape(16, 256))
    give, parts[1] = lax.optimization_barrier((give, parts[1]))
    give, weights = lax.optimization_barrier((give, weights))
    got = lax.ppermute(give, "c", [(0, 1), (1, 0)])

    par = jnp.stack([rec_gate, rec_cand, bias_gate])
    par = jnp.tile(lax.dynamic_slice(par, (0, mine * 8), (3, 8)), (1, 32))

    pre = project(place, keep, got, weights)
    late = [parts[0], parts[2]]
    pre, *late = lax.optimization_barrier((pre, *late))
    for i, part in zip((0, 2), late):
        parts[i] = moved(part, "zb", 4, SHIFTS[1 + i])
    pre = lax.all_to_all(pre.reshape(32, 32, 128), SEQ, 0, 0, tiled=True)
    state = newton(pre.reshape(16, 2, 2, 16, 128), par)
    half = jnp.stack(parts)
    peer = lax.ppermute(half, "c", [(0, 1), (1, 0)])
    state = lax.all_to_all(state.reshape(128, 8, 128), SEQ + ("zb",), 0, 0, tiled=True)
    sums, kept = output(place, state.reshape(1024, 128), own, half, peer)
    sums = lax.all_to_all(sums, "za", 0, 0, tiled=True)
    others = jnp.arange(4)[:, None, None] != lax.axis_index("za")
    total = kept + jnp.sum(jnp.where(others, sums.astype(F32), 0.0), axis=0)
    return total.astype(BF16)


def solution(mesh):
    fine = Mesh(mesh.devices.reshape(4, 4, 2, 4, 4), ("x", "y", "c", "za", "zb"))
    z = ("za", "zb")
    placed = (P(SEQ, z), P(), P(SEQ, z), P(SEQ, z), P(z), P(z), P(z), P(z, None))
    return jax.shard_map(per_device, mesh=fine, in_specs=placed, out_specs=P(SEQ, z), check_vma=False)
```
